512 devices in a mesh: pair: 64 (over y, x, core), ka: 8 (over z).
Axes of the slice: x: 4, y: 8, z: 8, core: 2. Of those that a mesh axis runs over, the one named last changes fastest.
Arguments:
- amplitudes: bfloat16 [32768, 4096], P('pair', 'ka'), may hold values from -6 to 6
- tile_mask: int32 [256, 32], P('pair', 'ka'), may hold values 0 or 1
- ladder_ints: bfloat16 [4096, 4096], P('ka', 'pair'), may hold values from -0.09375 to 0.09375
- cycle_right: bfloat16 [32768, 512], P('pair'), may hold values from -0.03125 to 0.03125
- cycle_left: bfloat16 [32768, 512], P('pair'), may hold values from -0.25 to 0.25
Outputs:
- residual: bfloat16 [32768, 4096], P('pair', 'ka')
The draws below stay inside these ranges and needn't reach their ends.
All inputs are finite; a program needn't handle non-finite values. No bound on the sum of `tile_mask` on one device may be relied on, other than what follows from the above.
Results may differ from the reference program's by a relative error of at most 0.015.
Values may be sent and summed in bfloat16 or wider, within the bound.
A program may use at most 64 MiB of HBM per device.

```python
import jax
import jax.numpy as jnp
from jax import lax

TB = 128
NO = 512
VT = 32
NV = 4096
NP = 32768
N_KA = 8


def set_ends(drawn, rng, smallest, top_value):
    shape = drawn.shape
    index_at = [jax.random.randint(jax.random.fold_in(rng, axis), (), 0, shape[axis]) for axis in range(len(shape))]
    drawn = drawn.at[tuple(index_at)].set(smallest)
    longest = shape.index(max(shape))
    index_at[longest] = (index_at[longest] + 1) % shape[longest]
    return drawn.at[tuple(index_at)].set(top_value)


def block_scale(stream_key, extent, shards, smallest, top_value):
    def one(axis_at, parts):
        steps = jax.random.uniform(jax.random.fold_in(jax.random.fold_in(stream_key, 6), axis_at), (parts,), jnp.float32, smallest / len(shards), top_value / len(shards))
        return jnp.repeat(jnp.exp(steps), extent[axis_at] // parts).reshape((-1,) + (1,) * (len(extent) - axis_at - 1))

    loudness = one(*shards[0])
    for cut in shards[1:]:
        loudness = loudness * one(*cut)
    return loudness


def noise(own_key, shape, scale, most, pieces=(), kind=jnp.bfloat16):
    drawn = jax.random.normal(own_key, shape, jnp.float32) * scale
    if len(pieces) > 0:
        drawn = block_scale(own_key, shape, pieces, -0.22, 0.18) * drawn
    return jnp.clip(drawn, min=-most, max=most).astype(kind)


def setup_inputs(seed: int = 0) -> dict:
    key_list = jax.random.split(jax.random.key(seed), 6)
    return {
        "amplitudes": noise(key_list[0], (NP, NV), 1.0, 6.0, ((0, 64), (1, 8))),
        "tile_mask": set_ends((jax.random.randint(key_list[1], (NP // TB, VT), 0, 4) < 3).astype(jnp.int32), jax.random.fold_in(key_list[1], 1), 0, 1),
        "ladder_ints": noise(key_list[2], (NV, NV), NV ** -0.5, 0.09375, ((0, 8), (1, 64))),
        "cycle_right": noise(key_list[3], (NP, NO), NP ** -0.5, 0.03125, ((0, 64),)),
        "cycle_left": noise(key_list[4], (NP, NO), NO ** -0.5, 0.25, ((0, 64),)),
    }


def reference(amplitudes, tile_mask, ladder_ints, cycle_right, cycle_left):
    rows_all = amplitudes.shape[0]
    tiles_row = tile_mask.shape[0]
    tiles_col = tile_mask.shape[1]
    masked = (amplitudes.reshape(tiles_row, TB, tiles_col, TB) * tile_mask[:, None, :, None].astype(jnp.bfloat16)).reshape(rows_all, NV)
    hole = lax.dot_general(masked, cycle_right, (((0,), (0,)), ((), ())), preferred_element_type=jnp.float32).astype(jnp.bfloat16)
    cycle_term = lax.dot_general(cycle_left, hole, (((1,), (1,)), ((), ())), preferred_element_type=jnp.float32)
    block_cols = NV // N_KA
    ladder_sum = jnp.zeros((rows_all, NV), jnp.float32)
    for index in range(N_KA):
        partial_block = jnp.dot(masked[:, index * block_cols:(index + 1) * block_cols], ladder_ints[index * block_cols:(index + 1) * block_cols, :], preferred_element_type=jnp.float32)
        rounded = lax.optimization_barrier(partial_block.astype(jnp.bfloat16))
        ladder_sum = ladder_sum + rounded.astype(jnp.float32)
    return (ladder_sum + cycle_term).astype(jnp.bfloat16)
```

```python
import jax
import jax.numpy as jnp
from jax import lax
from jax.experimental import pallas as pl
from jax.experimental.pallas import tpu as pltpu
from jax.sharding import PartitionSpec as P

MESH = pl.DeviceIdType.MESH
TB = 128
NB = 512
NX, NY, NZ = 4, 8, 8
LC = 64
CH = 128
NCH = NB // CH
HH = NB // 2
HP = HH // NY

bf16, f32 = jnp.bfloat16, jnp.float32
NT = (((1,), (1,)), ((), ()))
TN = (((0,), (0,)), ((), ()))


def kernel(
    mask_ref, amp_hbm, lad_hbm, right_hbm, left_hbm, out_ref,
    amp, lad, right, left, m, lt, la, lb, acc, part, hsend, hx, s1, hy, s2, hxx, hole,
    in_sem, m_ssem, m_rsem, l0_ssem, l0_rsem, l1_ssem, l1_rsem, l2_ssem, l2_rsem, l3_ssem, l3_rsem,
    h1_ssem, h1_rsem, h2_ssem, h2_rsem, h3_ssem, h3_rsem, h4_ssem, h4_rsem, h5_ssem, h5_rsem,
):
    p, z = lax.axis_index("pair"), lax.axis_index("ka")
    c, x, y = p % 2, (p // 2) % NX, p // (2 * NX)
    zt = (y - z + NZ) % NZ

    def dev(dx=0, dy=0, dz=0, dc=0):
        pair = ((y + dy) % NY) * (2 * NX) + ((x + dx) % NX) * 2 + (c + dc) % 2
        return (pair, (z + dz) % NZ)

    def rcopy(src, dst, ssem, rsem, device):
        return pltpu.make_async_remote_copy(
            src_ref=src, dst_ref=dst, send_sem=ssem, recv_sem=rsem, device_id=device, device_id_type=MESH)

    def rows(start, size):
        return pl.ds(pl.multiple_of(start, size), size)

    inputs = [pltpu.make_async_copy(a, b, in_sem.at[i]) for i, (a, b) in enumerate(
        ((amp_hbm, amp), (lad_hbm, lad), (right_hbm, right), (left_hbm, left)))]
    for copy in inputs:
        copy.start()

    barrier = pltpu.get_barrier_semaphore()
    partners = [dev(dz=1), dev(dz=-1), dev(dc=1)] + [dev(dx=d) for d in range(1, NX)] + [dev(dy=d) for d in range(1, NY)]
    for device in partners:
        pl.semaphore_signal(barrier, inc=1, device_id=device, device_id_type=MESH)

    @pl.when(zt != z)
    def _():
        pl.semaphore_signal(barrier, inc=1, device_id=(p, zt), device_id_type=MESH)

    inputs[0].wait()
    for r in range(NB // TB):
        for v in range(NB // TB):
            tile = amp[r * TB:(r + 1) * TB, v * TB:(v + 1) * TB].astype(f32)
            m[0, r * TB:(r + 1) * TB, v * TB:(v + 1) * TB] = (tile * mask_ref[r, v].astype(f32)).astype(bf16)
    pl.semaphore_wait(barrier, len(partners) + (zt != z).astype(jnp.int32))

    def m_copy(up, hop, ch):
        chunk = pl.ds(ch * CH, CH)
        src, dst = ((NZ - hop) % NZ, NZ - 1 - hop) if up else (hop, hop + 1)
        i = hop * NCH + ch
        return rcopy(m.at[src, chunk], m.at[dst, chunk], m_ssem.at[int(up), i], m_rsem.at[int(up), i], dev(dz=1 if up else -1))

    def m_chunks(up, hop):
        if hop < NZ // 2 - 1:
            return range(NCH)
        return range(NCH // 2) if up else range(NCH // 2, NCH)

    m_sent = []

    def m_send(up, hop, ch):
        copy = m_copy(up, hop, ch)
        copy.start()
        m_sent.append(copy)

    def m_forward(hop, ch):
        for up in (True, False):
            m_copy(up, hop - 1, ch).wait_recv()
            if ch in m_chunks(up, hop):
                m_send(up, hop, ch)

    for ch in range(NCH):
        for up in (True, False):
            m_send(up, 0, ch)

    q = 2 * x + c
    inputs[1].wait()
    lt[...] = lad[...].T
    l0a = rcopy(lt, la, l0_ssem.at[0], l0_rsem.at[0], dev(dy=z))
    l0b = rcopy(la, lb.at[z, rows(q * LC, LC)], l0_ssem.at[1], l0_rsem.at[1], (p, zt))

    @pl.when(z != 0)
    def _():
        l0a.start()

    inputs[2].wait()
    part[...] = lax.dot_general(m[0], right[...], TN, preferred_element_type=f32)
    hsend[...] = part[rows((1 - c) * HH, HH), :].astype(bf16)
    h1 = rcopy(hsend, hx, h1_ssem.at[0], h1_rsem.at[0], dev(dc=1))
    h1.start()

    @pl.when(z != 0)
    def _():
        l0a.wait_recv()

    @pl.when(z == 0)
    def _():
        la[...] = lt[...]

    @pl.when(zt != z)
    def _():
        l0b.start()

    @pl.when(zt == z)
    def _():
        lb[z, rows(q * LC, LC), :] = la[...]

    h1.wait_recv()
    s1[...] = (part[rows(c * HH, HH), :] + hx[...].astype(f32)).astype(bf16)
    h2 = []
    for d in range(1, NY):
        there = (y + d) % NY
        h2.append(rcopy(s1.at[rows(there * HP, HP)], hy.at[d], h2_ssem.at[d], h2_rsem.at[d], dev(dy=d)))
        h2[-1].start()

    @pl.when(zt != z)
    def _():
        l0b.wait_recv()

    order = (0, 1, 7, 2, 6, 3, 5, 4)

    def l_place(d):
        return lb.at[(y - d - z + 2 * NZ) % NZ, rows(q * LC, LC)]

    l1 = {}
    for d in order[1:]:
        l1[d] = rcopy(l_place(0), l_place(0), l1_ssem.at[d], l1_rsem.at[d], dev(dy=d))
        l1[d].start()
    l2 = {}

    def l2_send(d):
        for dx in (1, 3, 2):
            l2[d, dx] = rcopy(l_place(d), l_place(d), l2_ssem.at[dx, d], l2_rsem.at[dx, d], dev(dx=dx))
            l2[d, dx].start()

    l2_send(0)
    m_forward(1, 0)
    m_forward(1, 1)
    for d in order[1:3]:
        l1[d].wait_recv()
        l2_send(d)
    m_forward(1, 2)
    for copy in h2:
        copy.wait_recv()
    total = s1[rows(y * HP, HP), :].astype(f32)
    for d in range(1, NY):
        total += hy[d].astype(f32)
    s2[...] = total.astype(bf16)
    h3 = []
    for dx in range(1, NX):
        h3.append(rcopy(s2, hxx.at[dx], h3_ssem.at[dx], h3_rsem.at[dx], dev(dx=dx)))
        h3[-1].start()
    m_forward(1, 3)
    for d in order[3:5]:
        l1[d].wait_recv()
        l2_send(d)
    for copy in h3:
        copy.wait_recv()
    total = s2[...].astype(f32)
    for dx in range(1, NX):
        total += hxx[dx].astype(f32)
    mine = rows(c * HH + y * HP, HP)
    hole[mine, :] = total.astype(bf16)
    h4 = []
    for d in range(1, NY):
        h4.append(rcopy(hole.at[mine], hole.at[mine], h4_ssem.at[d], h4_rsem.at[d], dev(dy=d)))
        h4[-1].start()
    for d in order[5:]:
        l1[d].wait_recv()
        l2_send(d)
    m_forward(2, 0)
    m_forward(2, 1)
    m_forward(2, 2)
    for copy in h4:
        copy.wait_recv()
    half = rows(c * HH, HH)
    h5 = rcopy(hole.at[half], hole.at[half], h5_ssem.at[0], h5_rsem.at[0], dev(dc=1))
    h5.start()
    m_forward(2, 3)
    h5.wait_recv()
    inputs[3].wait()
    acc[...] = lax.dot_general(left[...], hole[...], NT, preferred_element_type=f32)

    l3 = []
    for dx in range(NX):
        if dx:
            for d in order:
                l2[d, dx].wait_recv()
        there = rows((2 * ((x - dx + NX) % NX) + c) * LC, LC)
        l3.append(rcopy(lb.at[:, there], lb.at[:, there], l3_ssem.at[dx], l3_rsem.at[dx], dev(dc=1)))
        l3[-1].start()
    for ch in range(NCH):
        m_forward(3, ch)
    for copy in l3:
        copy.wait_recv()

    @pl.loop(0, NZ - 1)
    def _(i):
        slot = jnp.where(i < NZ // 2, i, i + 1)
        acc[...] += lax.dot_general(m[slot], lb[(z + slot) % NZ], NT, preferred_element_type=f32)

    far = (z + NZ // 2) % NZ
    for i in range(NCH // 2):
        for up, ch in ((True, i), (False, NCH // 2 + i)):
            m_copy(up, NZ // 2 - 1, ch).wait_recv()
            chunk = pl.ds(ch * CH, CH)
            out_ref[chunk, :] = (acc[chunk, :] + lax.dot_general(
                m[NZ // 2, chunk], lb[far], NT, preferred_element_type=f32)).astype(bf16)

    for copy in m_sent + h2 + h3 + h4 + l3 + [h1, h5] + list(l1.values()) + list(l2.values()):
        copy.wait_send()

    @pl.when(z != 0)
    def _():
        l0a.wait_send()

    @pl.when(zt != z)
    def _():
        l0b.wait_send()


def body(amplitudes, tile_mask, ladder_ints, cycle_right, cycle_left):
    dma = pltpu.SemaphoreType.DMA
    pairs = lambda *shape: [dma(shape), dma(shape)]
    return pl.pallas_call(
        kernel,
        out_shape=jax.ShapeDtypeStruct((NB, NB), bf16),
        in_specs=[pl.BlockSpec(memory_space=pltpu.SMEM)] + [pl.BlockSpec(memory_space=pl.ANY)] * 4,
        out_specs=pl.BlockSpec(memory_space=pltpu.VMEM),
        scratch_shapes=[
            pltpu.VMEM((NB, NB), bf16),
            pltpu.VMEM((NB, LC), bf16),
            pltpu.VMEM((NB, NB), bf16),
            pltpu.VMEM((NB, NB), bf16),
            pltpu.VMEM((NZ, NB, NB), bf16),
            pltpu.VMEM((LC, NB), bf16),
            pltpu.VMEM((LC, NB), bf16),
            pltpu.VMEM((NZ, NB, NB), bf16),
            pltpu.VMEM((NB, NB), f32),
            pltpu.VMEM((NB, NB), f32),
            pltpu.VMEM((HH, NB), bf16),
            pltpu.VMEM((HH, NB), bf16),
            pltpu.VMEM((HH, NB), bf16),
            pltpu.VMEM((NY, HP, NB), bf16),
            pltpu.VMEM((HP, NB), bf16),
            pltpu.VMEM((NX, HP, NB), bf16),
            pltpu.VMEM((NB, NB), bf16),
            dma((4,)),
            *pairs(2, NZ // 2 * NCH),
            *pairs(2),
            *pairs(NY),
            *pairs(NX, NY),
            *pairs(NX),
            *pairs(1),
            *pairs(NY),
            *pairs(NX),
            *pairs(NY),
            *pairs(1),
        ],
        compiler_params=pltpu.CompilerParams(
            collective_id=0, has_side_effects=True, vmem_limit_bytes=48 * 2**20),
        cost_estimate=pl.CostEstimate(flops=2 * NB * NB * (NZ * NB + 2 * NB), bytes_accessed=5 * NB * NB * 2, transcendentals=0),
        name="residual_kernel",
    )(tile_mask, amplitudes, ladder_ints, cycle_right, cycle_left)


def solution(mesh):
    return jax.shard_map(
        body,
        mesh=mesh,
        in_specs=(
            P("pair", "ka"),
            P("pair", "ka"),
            P("ka", "pair"),
            P("pair", None),
            P("pair", None),
        ),
        out_specs=P("pair", "ka"),
        check_vma=False,
    )
```

```python
import jax
import jax.numpy as jnp
from jax import lax
from jax.experimental import pallas as pl
from jax.experimental.pallas import tpu as pltpu
from jax.sharding import PartitionSpec as P

MESH = pl.DeviceIdType.MESH
TB = 128
NB = 512
NX, NY, NZ = 4, 8, 8
LC = 64
CH = 64
NCH = NB // CH
EARLY = 6
HH = NB // 2
HP = HH // NY

bf16, f32 = jnp.bfloat16, jnp.float32
NT = (((1,), (1,)), ((), ()))
TN = (((0,), (0,)), ((), ()))


def kernel(
    mask_hbm, amp_hbm, lad_hbm, right_hbm, left_hbm, out_ref,
    mask, amp, lt, right, left, m, la, lb, acc, part, hsend, hx, s1, hy, s2, hxx, hole,
    relay_sem, in_sem, m_ssem, m_rsem, l0_ssem, l0_rsem, l1_ssem, l1_rsem, l2_ssem, l2_rsem, l3_ssem, l3_rsem,
    h1_ssem, h1_rsem, h2_ssem, h2_rsem, h3_ssem, h3_rsem, h4_ssem, h4_rsem, h5_ssem, h5_rsem,
):
    p, z = lax.axis_index("pair"), lax.axis_index("ka")
    c, x, y = p % 2, (p // 2) % NX, p // (2 * NX)
    zt = (y - z + NZ) % NZ

    def dev(dx=0, dy=0, dz=0, dc=0):
        pair = ((y + dy) % NY) * (2 * NX) + ((x + dx) % NX) * 2 + (c + dc) % 2
        return (pair, (z + dz) % NZ)

    def rcopy(src, dst, ssem, rsem, device):
        return pltpu.make_async_remote_copy(
            src_ref=src, dst_ref=dst, send_sem=ssem, recv_sem=rsem, device_id=device, device_id_type=MESH)

    def rows(start, size):
        return pl.ds(pl.multiple_of(start, size), size)

    inputs = [pltpu.make_async_copy(a, b, in_sem.at[i]) for i, (a, b) in enumerate(
        ((amp_hbm, amp), (lad_hbm, lt), (right_hbm, right), (left_hbm, left), (mask_hbm, mask)))]
    for copy in inputs[4:] + inputs[:4]:
        copy.start()

    barrier = pltpu.get_barrier_semaphore()
    neighbours = [dev(dz=1), dev(dz=-1), dev(dc=1), dev(dx=1), dev(dx=-1), dev(dy=1), dev(dy=-1)]
    for device in neighbours:
        pl.semaphore_signal(barrier, inc=1, device_id=device, device_id_type=MESH)

    inputs[4].wait()
    inputs[0].wait()
    for r in range(NB // TB):
        for v in range(NB // TB):
            tile = amp[r * TB:(r + 1) * TB, v * TB:(v + 1) * TB].astype(f32)
            m[0, r * TB:(r + 1) * TB, v * TB:(v + 1) * TB] = (tile * mask[r, v].astype(f32)).astype(bf16)
    pl.semaphore_wait(barrier, len(neighbours))

    def m_rows(up, ch):
        return pl.ds((ch if up else NCH - 1 - ch) * CH, CH)

    def m_copy(up, hop, ch):
        chunk = m_rows(up, ch)
        src, dst = ((NZ - hop) % NZ, NZ - 1 - hop) if up else (hop, hop + 1)
        i = hop * NCH + ch
        return rcopy(m.at[src, chunk], m.at[dst, chunk], m_ssem.at[int(up), i], m_rsem.at[int(up), i], dev(dz=1 if up else -1))

    m_sent = []

    def m_send(up, hop, ch):
        copy = m_copy(up, hop, ch)
        copy.start()
        m_sent.append(copy)

    def m_forward(hop, ch):
        for up in (True, False):
            m_copy(up, hop - 1, ch).wait_recv()
            if hop < NZ // 2 - 1 or ch < NCH // 2:
                m_send(up, hop, ch)

    def m_own(*chunks):
        for ch in chunks:
            for up in (True, False):
                m_send(up, 0, ch)

    m_own(*range(EARLY))

    def relay_signal(r):
        for axis in ("dy", "dz") + ("dx",) * (r == 1):
            for i, d in enumerate((r, -r)):
                pl.semaphore_signal(relay_sem.at["xyz".index(axis[1]), r, i], inc=1, device_id=dev(**{axis: d}), device_id_type=MESH)

    def relay_wait(r):
        for axis in ("dy", "dz") + ("dx",) * (r == 1):
            for i in range(2):
                pl.semaphore_wait(relay_sem.at["xyz".index(axis[1]), r, i], 1)

    l0a = rcopy(lt, la, l0_ssem.at[0], l0_rsem.at[0], dev(dy=z))
    l0b = rcopy(la, lb.at[z, x, c], l0_ssem.at[1], l0_rsem.at[1], (p, zt))

    def l0_first():
        inputs[1].wait()

        @pl.when(z != 0)
        def _():
            l0a.start()

    def l0_second():
        @pl.when(z != 0)
        def _():
            l0a.wait_recv()

        @pl.when(z == 0)
        def _():
            la[...] = lt[...]

        @pl.when(zt != z)
        def _():
            l0b.start()

        @pl.when(zt == z)
        def _():
            lb[z, x, c] = la[...]

    def l_place(d, dx=0):
        return lb.at[(y - d - z + 2 * NZ) % NZ, (x - dx + NX) % NX, c]

    def l1_copy(d):
        step = 1 if d <= NY // 2 else -1
        return rcopy(l_place(d - step), l_place(d - step), l1_ssem.at[d], l1_rsem.at[d], dev(dy=step))

    def l2_copy(d, dx):
        if dx != 2:
            return rcopy(l_place(d), l_place(d), l2_ssem.at[dx, d], l2_rsem.at[dx, d], dev(dx=dx))
        side = 1 if d % 2 else -1
        return rcopy(l_place(d, side), l_place(d, side), l2_ssem.at[dx, d], l2_rsem.at[dx, d], dev(dx=side))

    def l3_copy(d):
        there = lb.at[(y - d - z + 2 * NZ) % NZ, :, c]
        return rcopy(there, there, l3_ssem.at[d], l3_rsem.at[d], dev(dc=1))

    def l0_done():
        @pl.when(zt != z)
        def _():
            l0b.wait_recv()

    def l1_send(d):
        if d:
            l1_copy(d).wait_recv()
        else:
            l0_done()
            l1_copy(NY - 1).start()
        if d < NY // 2:
            l1_copy(d + 1).start()
        if d > NY // 2 + 1:
            l1_copy(d - 1).start()
        l2_copy(d, 1).start()
        l2_copy(d, 3).start()

    def l2_pass(d):
        l2_copy(d, 1 if d % 2 else 3).wait_recv()
        l2_copy(d, 2).start()

    def l3_send(d):
        l2_copy(d, 3 if d % 2 else 1).wait_recv()
        l2_copy(d, 2).wait_recv()
        l3_copy(d).start()

    def l3_done():
        for d in range(NY):
            l3_copy(d).wait_recv()

    def l_sent():
        for d in range(NY):
            if d:
                l1_copy(d).wait_send()
            for dx in range(1, NX):
                l2_copy(d, dx).wait_send()
            l3_copy(d).wait_send()

    def l0_sent():
        @pl.when(z != 0)
        def _():
            l0a.wait_send()

        @pl.when(zt != z)
        def _():
            l0b.wait_send()

    h1 = rcopy(hsend, hx, h1_ssem.at[0], h1_rsem.at[0], dev(dc=1))
    mine = rows(c * HH + y * HP, HP)
    half = rows(c * HH, HH)
    h5 = rcopy(hole.at[half], hole.at[half], h5_ssem.at[0], h5_rsem.at[0], dev(dc=1))

    def h2_copy(d):
        return rcopy(s1.at[rows((y + d) % NY * HP, HP)], hy.at[d], h2_ssem.at[d], h2_rsem.at[d], dev(dy=d))

    def h3_copy(dx):
        return rcopy(s2, hxx.at[dx], h3_ssem.at[dx], h3_rsem.at[dx], dev(dx=dx))

    def h4_copy(d):
        return rcopy(hole.at[mine], hole.at[mine], h4_ssem.at[d], h4_rsem.at[d], dev(dy=d))

    def h1_send():
        inputs[2].wait()
        part[...] = lax.dot_general(m[0], right[...], TN, preferred_element_type=f32)
        hsend[...] = part[rows((1 - c) * HH, HH), :].astype(bf16)
        h1.start()

    def h2_send():
        h1.wait_recv()
        s1[...] = (part[half, :] + hx[...].astype(f32)).astype(bf16)
        for d in range(1, NY):
            h2_copy(d).start()

    def h3_send():
        total = s1[rows(y * HP, HP), :].astype(f32)
        for d in range(1, NY):
            h2_copy(d).wait_recv()
            total += hy[d].astype(f32)
        s2[...] = total.astype(bf16)
        for dx in range(1, NX):
            h3_copy(dx).start()

    def h4_send():
        total = s2[...].astype(f32)
        for dx in range(1, NX):
            h3_copy(dx).wait_recv()
            total += hxx[dx].astype(f32)
        hole[mine, :] = total.astype(bf16)
        for d in range(1, NY):
            h4_copy(d).start()

    def h5_send():
        for d in range(1, NY):
            h4_copy(d).wait_recv()
        h5.start()

    def cycle():
        h5.wait_recv()
        inputs[3].wait()
        acc[...] = lax.dot_general(left[...], hole[...], NT, preferred_element_type=f32)

    def h_sent():
        h1.wait_send()
        for d in range(1, NY):
            h2_copy(d).wait_send()
            h4_copy(d).wait_send()
        for dx in range(1, NX):
            h3_copy(dx).wait_send()
        h5.wait_send()

    def ladder_block(slot):
        return lb[(z + slot) % NZ].reshape(NB, NB)

    def ladder():
        @pl.loop(0, NZ - 1)
        def _(i):
            slot = jnp.where(i < NZ // 2, i, i + 1)
            acc[...] += lax.dot_general(m[slot], ladder_block(slot), NT, preferred_element_type=f32)

    def last():
        block = ladder_block(NZ // 2)
        for ch in range(NCH // 2):
            for up in (True, False):
                m_copy(up, NZ // 2 - 1, ch).wait_recv()
                chunk = m_rows(up, ch)
                out_ref[chunk, :] = (acc[chunk, :] + lax.dot_general(
                    m[NZ // 2, chunk], block, NT, preferred_element_type=f32)).astype(bf16)

    def zm(hop, *chunks):
        for ch in chunks:
            m_forward(hop, ch)

    relay_signal(1)
    h1_send()
    relay_wait(1)
    relay_signal(2)
    relay_wait(2)
    l0_first()
    h2_send()
    l0_second()
    m_own(*range(EARLY, NCH))
    zm(1, 0, 1, 2, 3)
    zm(1, 4)
    l1_send(0)
    zm(1, 5, 6)
    l1_send(1)
    l1_send(7)
    zm(1, 7)
    l2_pass(0)
    l1_send(2)
    l1_send(6)
    zm(2, 0)
    h3_send()
    l2_pass(1)
    l2_pass(7)
    zm(2, 1, 2)
    l1_send(3)
    l1_send(5)
    zm(2, 3)
    l3_send(0)
    l2_pass(2)
    l2_pass(6)
    zm(2, 4)
    l1_send(4)
    h4_send()
    l3_send(1)
    l3_send(7)
    zm(2, 5, 6)
    l2_pass(3)
    l2_pass(5)
    l3_send(2)
    l3_send(6)
    zm(2, 7)
    l2_pass(4)
    zm(3, 0, 1)
    l3_send(3)
    l3_send(5)
    zm(3, 2)
    l3_send(4)
    zm(3, 3)
    h5_send()
    zm(3, 4, 5)
    cycle()
    l3_done()
    zm(3, 6, 7)
    ladder()
    last()
    for copy in m_sent:
        copy.wait_send()
    l0_sent()
    l_sent()
    h_sent()


def body(amplitudes, tile_mask, ladder_ints, cycle_right, cycle_left):
    dma = pltpu.SemaphoreType.DMA
    pairs = lambda *shape: [dma(shape), dma(shape)]
    return pl.pallas_call(
        kernel,
        out_shape=jax.ShapeDtypeStruct((NB, NB), bf16),
        in_specs=[pl.BlockSpec(memory_space=pl.ANY)] * 5,
        out_specs=pl.BlockSpec(memory_space=pltpu.VMEM),
        scratch_shapes=[
            pltpu.SMEM((NB // TB, NB // TB), jnp.int32),
            pltpu.VMEM((NB, NB), bf16),
            pltpu.VMEM((LC, NB), bf16),
            pltpu.VMEM((NB, NB), bf16),
            pltpu.VMEM((NB, NB), bf16),
            pltpu.VMEM((NZ, NB, NB), bf16),
            pltpu.VMEM((LC, NB), bf16),
            pltpu.VMEM((NZ, NX, 2, LC, NB), bf16),
            pltpu.VMEM((NB, NB), f32),
            pltpu.VMEM((NB, NB), f32),
            pltpu.VMEM((HH, NB), bf16),
            pltpu.VMEM((HH, NB), bf16),
            pltpu.VMEM((HH, NB), bf16),
            pltpu.VMEM((NY, HP, NB), bf16),
            pltpu.VMEM((HP, NB), bf16),
            pltpu.VMEM((NX, HP, NB), bf16),
            pltpu.VMEM((NB, NB), bf16),
            pltpu.SemaphoreType.REGULAR((3, 4, 2)),
            dma((5,)),
            *pairs(2, NZ // 2 * NCH),
            *pairs(2),
            *pairs(NY),
            *pairs(NX, NY),
            *pairs(NY),
            *pairs(1),
            *pairs(NY),
            *pairs(NX),
            *pairs(NY),
            *pairs(1),
        ],
        compiler_params=pltpu.CompilerParams(
            collective_id=0, has_side_effects=True, vmem_limit_bytes=63 * 2**20),
        cost_estimate=pl.CostEstimate(flops=2 * NB * NB * (NZ * NB + 2 * NB), bytes_accessed=5 * NB * NB * 2, transcendentals=0),
        name="residual_kernel",
    )(tile_mask, amplitudes, ladder_ints.T, cycle_right, cycle_left)


def solution(mesh):
    return jax.shard_map(
        body,
        mesh=mesh,
        in_specs=(
            P("pair", "ka"),
            P("pair", "ka"),
            P("ka", "pair"),
            P("pair", None),
            P("pair", None),
        ),
        out_specs=P("pair", "ka"),
        check_vma=False,
    )
```

```python
import jax
import jax.numpy as jnp
from jax import lax
from jax.experimental import pallas as pl
from jax.experimental.pallas import tpu as pltpu
from jax.sharding import PartitionSpec as P

MESH = pl.DeviceIdType.MESH
TB = 128
NB = 512
NX, NY, NZ = 4, 8, 8
LC = 64
CH = 128
NCH = NB // CH
EARLY = 2
HH = NB // 2
HP = HH // NY

bf16, f32 = jnp.bfloat16, jnp.float32
NT = (((1,), (1,)), ((), ()))
TN = (((0,), (0,)), ((), ()))


def kernel(
    mask_hbm, amp_hbm, lad_hbm, right_hbm, left_hbm, out_hbm,
    mask, amp, lt, right, left, m, la, lb, acc, part, hsend, hx, s1, hy, s2, hxx, hole, out,
    ack, in_sem, out_sem, m_ssem, m_rsem, l0_ssem, l0_rsem, l1_ssem, l1_rsem, l2_ssem, l2_rsem, l3_ssem, l3_rsem,
    h1_ssem, h1_rsem, h2_ssem, h2_rsem, h3_ssem, h3_rsem, h4_ssem, h4_rsem, h5_ssem, h5_rsem,
):
    p, z = lax.axis_index("pair"), lax.axis_index("ka")
    c, x, y = p % 2, (p // 2) % NX, p // (2 * NX)
    zt = (y - z + NZ) % NZ

    def dev(dx=0, dy=0, dz=0, dc=0):
        pair = ((y + dy) % NY) * (2 * NX) + ((x + dx) % NX) * 2 + (c + dc) % 2
        return (pair, (z + dz) % NZ)

    def rcopy(src, dst, ssem, rsem, device):
        return pltpu.make_async_remote_copy(
            src_ref=src, dst_ref=dst, send_sem=ssem, recv_sem=rsem, device_id=device, device_id_type=MESH)

    def drain(ref, sem):
        pltpu.make_async_copy(ref, ref, sem).wait()

    def rows(start, size):
        return pl.ds(pl.multiple_of(start, size), size)

    mask_in = pltpu.make_async_copy(mask_hbm, mask, in_sem.at[0])
    inputs = [pltpu.make_async_copy(a, b, in_sem.at[1 + i]) for i, (a, b) in enumerate(
        ((lad_hbm, lt), (right_hbm, right), (left_hbm, left)))]
    amp_in = [pltpu.make_async_copy(amp_hbm.at[pl.ds(i * CH, CH)], amp.at[pl.ds(i * CH, CH)], in_sem.at[4 + i]) for i in range(NCH)]
    from_ends = [i for j in range(NCH // 2) for i in (j, NCH - 1 - j)]
    mask_in.start()
    amp_in[from_ends[0]].start()
    amp_in[from_ends[1]].start()

    def rank(v):
        return jnp.where(v <= NY // 2, 2 * v, 2 * (NY - v) + 1)

    partners = {
        ("z", 1): (dev(dz=1), (z + 1) % NZ > z, None, ("z", -1)),
        ("z", -1): (dev(dz=-1), (z + NZ - 1) % NZ > z, None, ("z", 1)),
        ("t", 0): ((p, zt), zt > z, zt != z, ("t", 0)),
        ("c", 1): (dev(dc=1), c == 1, None, ("c", 1)),
    }
    for d in range(1, NX):
        partners["x", d] = (dev(dx=d), (x + d) % NX > x, None, ("x", NX - d))
    for d in range(1, NY):
        partners["y", d] = (dev(dy=d), rank((y + d) % NY) > rank(y), None, ("y", NY - d))
    ack_of = {name: i for i, name in enumerate(partners)}

    barrier = pltpu.get_barrier_semaphore()
    earlier = 0
    for device, later, valid, _ in partners.values():
        @pl.when(later)
        def _():
            pl.semaphore_signal(barrier, inc=1, device_id=device, device_id_type=MESH)

        before = jnp.logical_not(later)
        if valid is not None:
            before = jnp.logical_and(before, valid)
        earlier += before.astype(jnp.int32)

    def answer():
        @pl.when(earlier > 0)
        def _():
            pl.semaphore_wait(barrier, earlier)

        for device, later, valid, there in partners.values():
            before = jnp.logical_not(later)
            if valid is not None:
                before = jnp.logical_and(before, valid)

            @pl.when(before)
            def _():
                pl.semaphore_signal(ack.at[ack_of[there]], inc=1, device_id=device, device_id_type=MESH)

    def met(axis):
        for name, (_, later, _, _) in partners.items():
            if name[0] == axis:
                @pl.when(later)
                def _():
                    pl.semaphore_wait(ack.at[ack_of[name]], 1)

    for i in from_ends[2:]:
        amp_in[i].start()
    for copy in inputs:
        copy.start()

    def masked(i):
        amp_in[i].wait()
        for v in range(NB // TB):
            here = (slice(i * CH, (i + 1) * CH), slice(v * TB, (v + 1) * TB))
            m[(0, *here)] = (amp[here].astype(f32) * mask[i * CH // TB, v].astype(f32)).astype(bf16)

    mask_in.wait()
    masked(from_ends[0])
    masked(from_ends[1])
    answer()
    met("z")

    def m_rows(up, ch):
        return pl.ds((ch if up else NCH - 1 - ch) * CH, CH)

    def m_copy(up, hop, ch):
        chunk = m_rows(up, ch)
        src, dst = ((NZ - hop) % NZ, NZ - 1 - hop) if up else (hop, hop + 1)
        i = hop * NCH + ch
        return rcopy(m.at[src, chunk], m.at[dst, chunk], m_ssem.at[0], m_rsem.at[int(up), i], dev(dz=1 if up else -1))

    def m_send(up, hop, ch):
        m_copy(up, hop, ch).start()

    def m_forward(hop, ch):
        for up in (True, False):
            m_copy(up, hop - 1, ch).wait_recv()
            if hop < NZ // 2 - 1 or ch < NCH // 2:
                m_send(up, hop, ch)

    def m_own(*chunks):
        for ch in chunks:
            for up in (True, False):
                m_send(up, 0, ch)

    m_own(0)
    for i in range(1, NCH // 2):
        masked(from_ends[2 * i])
        masked(from_ends[2 * i + 1])
        if i < EARLY:
            m_own(i)
    m_own(*range(NCH // 2, EARLY))

    l0a = rcopy(lt, la, l0_ssem.at[0], l0_rsem.at[0], dev(dy=z))
    l0b = rcopy(la, lb.at[z, x, c], l0_ssem.at[1], l0_rsem.at[1], (p, zt))

    def l0_first():
        inputs[0].wait()

        @pl.when(z != 0)
        def _():
            l0a.start()

    def l0_second():
        @pl.when(z != 0)
        def _():
            l0a.wait_recv()

        @pl.when(z == 0)
        def _():
            la[...] = lt[...]

        @pl.when(zt != z)
        def _():
            l0b.start()

        @pl.when(zt == z)
        def _():
            lb[z, x, c] = la[...]

    def l_place(d, dx=0):
        return lb.at[(y - d - z + 2 * NZ) % NZ, (x - dx + NX) % NX, c]

    def l1_copy(d):
        if d == NY // 2:
            src, step = l_place(jnp.where(c == 0, 2, NY - 2)), jnp.where(c == 0, 2, NY - 2)
        else:
            step = {1: 1, 2: 2, 3: 1, 5: NY - 1, 6: NY - 2, 7: NY - 1}[d]
            src = l_place((d - step + NY) % NY)
        return rcopy(src, src, l1_ssem.at[0], l1_rsem.at[d], dev(dy=step))

    def l2_copy(d, dx):
        side = 1 if d % 2 else NX - 1
        src, step = (l_place(d, side), side) if dx == 2 else (l_place(d), dx)
        return rcopy(src, src, l2_ssem.at[0], l2_rsem.at[0 if dx == side else 1, d], dev(dx=step))

    def l3_copy(d):
        there = lb.at[(y - d - z + 2 * NZ) % NZ, :, c]
        return rcopy(there, there, l3_ssem.at[0], l3_rsem.at[0], dev(dc=1))

    def l0_done():
        @pl.when(zt != z)
        def _():
            l0b.wait_recv()

    def l1_send(d):
        if d:
            l1_copy(d).wait_recv()
        else:
            l0_done()
        for further in {0: (1, 7, 2, 6), 2: (3,), 6: (5, 4)}.get(d, ()):
            l1_copy(further).start()
        l2_copy(d, 1).start()
        l2_copy(d, 3).start()

    def l2_pass(d):
        l2_copy(d, 1 if d % 2 else 3).wait_recv()
        l2_copy(d, 2).start()

    def l3_send(d):
        drain(lb.at[0, pl.ds(0, 2), 0], l2_rsem.at[1, d])
        l3_copy(d).start()

    def l3_done():
        drain(lb.at[:, :, 0], l3_rsem.at[0])

    def l_sent():
        drain(lb.at[pl.ds(0, NY - 1), 0, 0], l1_ssem.at[0])
        drain(lb.at[:, pl.ds(0, NX - 1), 0], l2_ssem.at[0])
        drain(lb.at[:, :, 0], l3_ssem.at[0])

    def l0_sent():
        @pl.when(z != 0)
        def _():
            l0a.wait_send()

        @pl.when(zt != z)
        def _():
            l0b.wait_send()

    h1 = rcopy(hsend, hx, h1_ssem.at[0], h1_rsem.at[0], dev(dc=1))
    mine = rows(c * HH + y * HP, HP)
    half = rows(c * HH, HH)
    h5 = rcopy(hole.at[half], hole.at[half], h5_ssem.at[0], h5_rsem.at[0], dev(dc=1))

    def h2_copy(d):
        return rcopy(s1.at[rows((y + d) % NY * HP, HP)], hy.at[d], h2_ssem.at[0], h2_rsem.at[0], dev(dy=d))

    def h3_copy(dx):
        return rcopy(s2, hxx.at[dx], h3_ssem.at[0], h3_rsem.at[0], dev(dx=dx))

    def h4_copy(d):
        return rcopy(hole.at[mine], hole.at[mine], h4_ssem.at[0], h4_rsem.at[0], dev(dy=d))

    def h1_send():
        inputs[1].wait()
        part[...] = lax.dot_general(m[0], right[...], TN, preferred_element_type=f32)
        hsend[...] = part[rows((1 - c) * HH, HH), :].astype(bf16)
        h1.start()

    def h2_send():
        h1.wait_recv()
        s1[...] = (part[half, :] + hx[...].astype(f32)).astype(bf16)
        for d in range(1, NY):
            h2_copy(d).start()

    def h3_send():
        drain(hy.at[pl.ds(1, NY - 1)], h2_rsem.at[0])
        total = s1[rows(y * HP, HP), :].astype(f32)
        for d in range(1, NY):
            total += hy[d].astype(f32)
        s2[...] = total.astype(bf16)
        for dx in range(1, NX):
            h3_copy(dx).start()

    def h4_send():
        drain(hxx.at[pl.ds(1, NX - 1)], h3_rsem.at[0])
        total = s2[...].astype(f32)
        for dx in range(1, NX):
            total += hxx[dx].astype(f32)
        hole[mine, :] = total.astype(bf16)
        for d in range(1, NY):
            h4_copy(d).start()

    def h5_send():
        drain(hy.at[pl.ds(1, NY - 1)], h4_rsem.at[0])
        h5.start()

    def cycle():
        h5.wait_recv()
        inputs[2].wait()
        acc[...] = lax.dot_general(left[...], hole[...], NT, preferred_element_type=f32)

    def h_sent():
        h1.wait_send()
        drain(hy.at[pl.ds(1, NY - 1)], h2_ssem.at[0])
        drain(hxx.at[pl.ds(1, NX - 1)], h3_ssem.at[0])
        drain(hy.at[pl.ds(1, NY - 1)], h4_ssem.at[0])
        h5.wait_send()

    def ladder_block(slot):
        return lb[(z + slot) % NZ].reshape(NB, NB)

    def ladder(n, first, step):
        @pl.loop(0, n)
        def _(i):
            slot = (first + step * i) % NZ
            acc[...] += lax.dot_general(m[slot], ladder_block(slot), NT, preferred_element_type=f32)

    def last():
        block = ladder_block(NZ // 2)
        for ch in range(NCH // 2):
            for up in (True, False):
                m_copy(up, NZ // 2 - 1, ch).wait_recv()
                chunk = m_rows(up, ch)
                out[chunk, :] = (acc[chunk, :] + lax.dot_general(
                    m[NZ // 2, chunk], block, NT, preferred_element_type=f32)).astype(bf16)
                pltpu.make_async_copy(out.at[chunk], out_hbm.at[chunk], out_sem.at[0]).start()

    def zm(hop, *chunks):
        for ch in chunks:
            m_forward(hop, ch)

    met("y")
    l0_first()
    met("c")
    h1_send()
    h2_send()
    zm(1, 0)
    met("t")
    l0_second()
    m_own(*range(EARLY, NCH))
    zm(1, 1)
    met("x")
    l1_send(0)
    zm(1, 2)
    l1_send(1)
    l1_send(7)
    l2_pass(0)
    l1_send(2)
    l1_send(6)
    zm(1, 3)
    h3_send()
    l2_pass(1)
    l2_pass(7)
    zm(2, 0)
    l1_send(3)
    l1_send(5)
    l3_send(0)
    l1_send(4)
    l2_pass(2)
    l2_pass(6)
    zm(2, 1)
    h4_send()
    l3_send(1)
    l3_send(7)
    l2_pass(3)
    l2_pass(5)
    l2_pass(4)
    zm(2, 2)
    l3_send(2)
    l3_send(6)
    zm(2, 3)
    l3_send(3)
    l3_send(5)
    l3_send(4)
    h5_send()
    zm(3, 0)
    cycle()
    zm(3, 1)
    l3_done()
    ladder(5, 6, 1)
    zm(3, 2, 3)
    ladder(2, 3, 2)
    last()
    drain(out, out_sem.at[0])
    drain(m.at[pl.ds(0, NZ - 1)], m_ssem.at[0])
    l0_sent()
    l_sent()
    h_sent()


def body(amplitudes, tile_mask, ladder_ints, cycle_right, cycle_left):
    dma = pltpu.SemaphoreType.DMA
    return pl.pallas_call(
        kernel,
        out_shape=jax.ShapeDtypeStruct((NB, NB), bf16),
        in_specs=[pl.BlockSpec(memory_space=pl.ANY)] * 5,
        out_specs=pl.BlockSpec(memory_space=pl.ANY),
        scratch_shapes=[
            pltpu.SMEM((NB // TB, NB // TB), jnp.int32),
            pltpu.VMEM((NB, NB), bf16),
            pltpu.VMEM((LC, NB), bf16),
            pltpu.VMEM((NB, NB), bf16),
            pltpu.VMEM((NB, NB), bf16),
            pltpu.VMEM((NZ, NB, NB), bf16),
            pltpu.VMEM((LC, NB), bf16),
            pltpu.VMEM((NZ, NX, 2, LC, NB), bf16),
            pltpu.VMEM((NB, NB), f32),
            pltpu.VMEM((NB, NB), f32),
            pltpu.VMEM((HH, NB), bf16),
            pltpu.VMEM((HH, NB), bf16),
            pltpu.VMEM((HH, NB), bf16),
            pltpu.VMEM((NY, HP, NB), bf16),
            pltpu.VMEM((HP, NB), bf16),
            pltpu.VMEM((NX, HP, NB), bf16),
            pltpu.VMEM((NB, NB), bf16),
            pltpu.VMEM((NB, NB), bf16),
            pltpu.SemaphoreType.REGULAR((4 + NX - 1 + NY - 1,)),
            dma((4 + NCH,)),
            dma((1,)),
            dma((1,)), dma((2, NZ // 2 * NCH - NCH // 2)),
            dma((2,)), dma((2,)),
            dma((1,)), dma((NY,)),
            dma((1,)), dma((2, NY)),
            dma((1,)), dma((1,)),
            *[dma((1,))] * 10,
        ],
        compiler_params=pltpu.CompilerParams(
            collective_id=0, has_side_effects=True, vmem_limit_bytes=64 * 2**20),
        cost_estimate=pl.CostEstimate(flops=2 * NB * NB * (NZ * NB + 2 * NB), bytes_accessed=5 * NB * NB * 2, transcendentals=0),
        name="residual_kernel",
    )(tile_mask, amplitudes, ladder_ints.T, cycle_right, cycle_left)


def solution(mesh):
    return jax.shard_map(
        body,
        mesh=mesh,
        in_specs=(
            P("pair", "ka"),
            P("pair", "ka"),
            P("ka", "pair"),
            P("pair", None),
            P("pair", None),
        ),
        out_specs=P("pair", "ka"),
        check_vma=False,
    )
```

```python
import jax
import jax.numpy as jnp
from jax import lax
from jax.experimental import pallas as pl
from jax.experimental.pallas import tpu as pltpu
from jax.sharding import PartitionSpec as P

MESH = pl.DeviceIdType.MESH
TB = 128
NB = 512
NX, NY, NZ = 4, 8, 8
LC = 64
CH = 128
NCH = NB // CH
BESIDE = (1, NY - 1)
EARLY = 2
HH = NB // 2
HQ = HH // NX
HP, HW = HQ // 4, NB // 2

bf16, f32 = jnp.bfloat16, jnp.float32
NT = (((1,), (1,)), ((), ()))
TN = (((0,), (0,)), ((), ()))


def kernel(
    mask_hbm, amp_hbm, lad_hbm, right_hbm, left_hbm, out_hbm,
    mask, amp, lt, right, left, m, la, lb, acc, part, hsend, hx, s1, hy, s2, hxx, hole, out,
    ack, in_sem, out_sem, m_ssem, m_rsem, l0_ssem, l0_rsem, l1_ssem, l1_rsem, l2_ssem, l2_rsem, l3_ssem, l3_rsem,
    h1_ssem, h1_rsem, h2_ssem, h2_rsem, h3_ssem, h3_rsem, h4_ssem, h4_rsem, h5_ssem, h5_rsem, h6_ssem, h6_rsem,
):
    p, z = lax.axis_index("pair"), lax.axis_index("ka")
    c, x, y = p % 2, (p // 2) % NX, p // (2 * NX)
    zt = (y - z + NZ) % NZ

    def dev(dx=0, dy=0, dz=0, dc=0):
        pair = ((y + dy) % NY) * (2 * NX) + ((x + dx) % NX) * 2 + (c + dc) % 2
        return (pair, (z + dz) % NZ)

    def rcopy(src, dst, ssem, rsem, device):
        return pltpu.make_async_remote_copy(
            src_ref=src, dst_ref=dst, send_sem=ssem, recv_sem=rsem, device_id=device, device_id_type=MESH)

    def drain(ref, sem):
        pltpu.make_async_copy(ref, ref, sem).wait()

    def rows(start, size):
        return pl.ds(pl.multiple_of(start, size), size)

    mask_in = pltpu.make_async_copy(mask_hbm, mask, in_sem.at[0])
    inputs = [pltpu.make_async_copy(a, b, in_sem.at[1 + i]) for i, (a, b) in enumerate(
        ((lad_hbm, lt), (right_hbm, right), (left_hbm, left)))]
    amp_in = [pltpu.make_async_copy(amp_hbm.at[pl.ds(i * CH, CH)], amp.at[pl.ds(i * CH, CH)], in_sem.at[4 + i]) for i in range(NCH)]
    from_ends = [i for j in range(NCH // 2) for i in (j, NCH - 1 - j)]
    mask_in.start()
    amp_in[from_ends[0]].start()
    amp_in[from_ends[1]].start()

    def rank(v):
        return jnp.where(v <= NY // 2, 2 * v, 2 * (NY - v) + 1)

    partners = {
        ("z", 1): (dev(dz=1), (z + 1) % NZ > z, None, ("z", -1)),
        ("z", -1): (dev(dz=-1), (z + NZ - 1) % NZ > z, None, ("z", 1)),
        ("t", 0): ((p, zt), zt > z, zt != z, ("t", 0)),
        ("c", 1): (dev(dc=1), c == 1, None, ("c", 1)),
    }
    for d in range(1, NX):
        partners["x", d] = (dev(dx=d), (x + d) % NX > x, None, ("x", NX - d))
    for d in range(1, NY):
        partners["y", d] = (dev(dy=d), rank((y + d) % NY) > rank(y), None, ("y", NY - d))
    ack_of = {name: i for i, name in enumerate(partners)}

    barrier = pltpu.get_barrier_semaphore()
    earlier = 0
    for device, later, valid, _ in partners.values():
        @pl.when(later)
        def _():
            pl.semaphore_signal(barrier, inc=1, device_id=device, device_id_type=MESH)

        before = jnp.logical_not(later)
        if valid is not None:
            before = jnp.logical_and(before, valid)
        earlier += before.astype(jnp.int32)

    def answer():
        @pl.when(earlier > 0)
        def _():
            pl.semaphore_wait(barrier, earlier)

        for device, later, valid, there in partners.values():
            before = jnp.logical_not(later)
            if valid is not None:
                before = jnp.logical_and(before, valid)

            @pl.when(before)
            def _():
                pl.semaphore_signal(ack.at[ack_of[there]], inc=1, device_id=device, device_id_type=MESH)

    def met(axis):
        for name, (_, later, _, _) in partners.items():
            if name[0] == axis:
                @pl.when(later)
                def _():
                    pl.semaphore_wait(ack.at[ack_of[name]], 1)

    for i in from_ends[2:]:
        amp_in[i].start()
    for copy in inputs:
        copy.start()

    def masked(i):
        amp_in[i].wait()
        for v in range(NB // TB):
            here = (slice(i * CH, (i + 1) * CH), slice(v * TB, (v + 1) * TB))
            m[(0, *here)] = (amp[here].astype(f32) * mask[i * CH // TB, v].astype(f32)).astype(bf16)

    mask_in.wait()
    masked(from_ends[0])
    masked(from_ends[1])
    answer()
    met("z")

    def m_rows(up, ch):
        return pl.ds((ch if up else NCH - 1 - ch) * CH, CH)

    def m_copy(up, hop, ch):
        chunk = m_rows(up, ch)
        src, dst = ((NZ - hop) % NZ, NZ - 1 - hop) if up else (hop, hop + 1)
        i = hop * NCH + ch
        return rcopy(m.at[src, chunk], m.at[dst, chunk], m_ssem.at[0], m_rsem.at[int(up), i], dev(dz=1 if up else -1))

    def m_send(up, hop, ch):
        m_copy(up, hop, ch).start()

    def m_forward(hop, ch):
        for up in (True, False):
            m_copy(up, hop - 1, ch).wait_recv()
            if hop < NZ // 2 - 1 or ch < NCH // 2:
                m_send(up, hop, ch)

    def m_own(*chunks):
        for ch in chunks:
            for up in (True, False):
                m_send(up, 0, ch)

    m_own(0)
    for i in range(1, NCH // 2):
        masked(from_ends[2 * i])
        masked(from_ends[2 * i + 1])
        if i < EARLY:
            m_own(i)
    m_own(*range(NCH // 2, EARLY))

    l0a = rcopy(lt, la, l0_ssem.at[0], l0_rsem.at[0], dev(dy=z))
    l0b = rcopy(la, lb.at[z, x, c], l0_ssem.at[1], l0_rsem.at[1], (p, zt))

    def l0_first():
        inputs[0].wait()

        @pl.when(z != 0)
        def _():
            l0a.start()

    def l0_second():
        @pl.when(z != 0)
        def _():
            l0a.wait_recv()

        @pl.when(z == 0)
        def _():
            la[...] = lt[...]

        @pl.when(zt != z)
        def _():
            l0b.start()

        @pl.when(zt == z)
        def _():
            lb[z, x, c] = la[...]

    def l_place(d, dx=0):
        return lb.at[(y - d - z + 2 * NZ) % NZ, (x - dx + NX) % NX, c]

    def l1_copy(d):
        if d == NY // 2:
            src, step = l_place(jnp.where(c == 0, 2, NY - 2)), jnp.where(c == 0, 2, NY - 2)
        else:
            step = {1: 1, 2: 2, 3: 1, 5: NY - 1, 6: NY - 2, 7: NY - 1}[d]
            src = l_place((d - step + NY) % NY)
        return rcopy(src, src, l1_ssem.at[0], l1_rsem.at[d], dev(dy=step))

    def l2_copy(d, dx):
        side = 1 if d % 2 else NX - 1
        src, step = (l_place(d, side), side) if dx == 2 else (l_place(d), dx)
        return rcopy(src, src, l2_ssem.at[0], l2_rsem.at[0 if dx == side else 1, d], dev(dx=step))

    def l2_beside(d, dx):
        return rcopy(l_place(0, dx), l_place(0, dx), l2_ssem.at[0], l2_rsem.at[1, d], dev(dy=d))

    def l3_copy(d):
        there = lb.at[(y - d - z + 2 * NZ) % NZ, :, c]
        return rcopy(there, there, l3_ssem.at[0], l3_rsem.at[0], dev(dc=1))

    def l0_done():
        @pl.when(zt != z)
        def _():
            l0b.wait_recv()

    def l1_send(d):
        if d:
            l1_copy(d).wait_recv()
        else:
            l0_done()
        for further in {0: (1, 7, 2, 6), 2: (3,), 6: (5, 4)}.get(d, ()):
            l1_copy(further).start()
        if d not in BESIDE:
            l2_copy(d, 1).start()
            l2_copy(d, 3).start()

    def l2_pass(d):
        l2_copy(d, 1 if d % 2 else 3).wait_recv()
        l2_copy(d, 2).start()

    def l3_send(d):
        drain(lb.at[0, pl.ds(0, 3 if d in BESIDE else 2), 0], l2_rsem.at[1, d])
        l3_copy(d).start()
        if d == 0:
            for beside in BESIDE:
                for dx in range(1, NX):
                    l2_beside(beside, dx).start()

    def l3_done():
        drain(lb.at[:, :, 0], l3_rsem.at[0])

    def l_sent():
        drain(lb.at[pl.ds(0, NY - 1), 0, 0], l1_ssem.at[0])
        drain(lb.at[:, pl.ds(0, NX - 1), 0], l2_ssem.at[0])
        drain(lb.at[:, :, 0], l3_ssem.at[0])

    def l0_sent():
        @pl.when(z != 0)
        def _():
            l0a.wait_send()

        @pl.when(zt != z)
        def _():
            l0b.wait_send()

    h1 = rcopy(hsend, hx, h1_ssem.at[0], h1_rsem.at[0], dev(dc=1))
    half = rows(c * HH, HH)
    quarter = rows(c * HH + x * HQ, HQ)
    h6 = rcopy(hole.at[half], hole.at[half], h6_ssem.at[0], h6_rsem.at[0], dev(dc=1))

    def piece(v):
        return rows(v // 2 * HP, HP), rows(v % 2 * HW, HW)

    mine = (rows(c * HH + x * HQ + y // 2 * HP, HP), rows(y % 2 * HW, HW))

    def h2_copy(dx):
        return rcopy(s1.at[rows((x + dx) % NX * HQ, HQ)], hxx.at[dx], h2_ssem.at[0], h2_rsem.at[0], dev(dx=dx))

    def h3_copy(d):
        return rcopy(s2.at[piece((y + d) % NY)], hy.at[d], h3_ssem.at[0], h3_rsem.at[0], dev(dy=d))

    def h4_copy(d):
        return rcopy(hole.at[mine], hole.at[mine], h4_ssem.at[0], h4_rsem.at[0], dev(dy=d))

    def h5_copy(dx):
        return rcopy(hole.at[quarter], hole.at[quarter], h5_ssem.at[0], h5_rsem.at[0], dev(dx=dx))

    def h1_send():
        inputs[1].wait()
        part[...] = lax.dot_general(m[0], right[...], TN, preferred_element_type=f32)
        hsend[...] = part[rows((1 - c) * HH, HH), :].astype(bf16)
        h1.start()

    def h2_send():
        h1.wait_recv()
        s1[...] = (part[half, :] + hx[...].astype(f32)).astype(bf16)
        for dx in range(1, NX):
            h2_copy(dx).start()

    def h3_send():
        drain(hxx.at[pl.ds(1, NX - 1)], h2_rsem.at[0])
        total = s1[rows(x * HQ, HQ), :].astype(f32)
        for dx in range(1, NX):
            total += hxx[dx].astype(f32)
        s2[...] = total.astype(bf16)
        for d in range(1, NY):
            h3_copy(d).start()

    def h4_send():
        drain(hy.at[pl.ds(1, NY - 1)], h3_rsem.at[0])
        total = s2[piece(y)].astype(f32)
        for d in range(1, NY):
            total += hy[d].astype(f32)
        hole[mine] = total.astype(bf16)
        for d in range(1, NY):
            h4_copy(d).start()

    def h5_send():
        drain(hy.at[pl.ds(1, NY - 1)], h4_rsem.at[0])
        for dx in range(1, NX):
            h5_copy(dx).start()

    def h6_send():
        drain(hxx.at[pl.ds(1, NX - 1)], h5_rsem.at[0])
        h6.start()

    def cycle():
        h6.wait_recv()
        inputs[2].wait()
        acc[...] = lax.dot_general(left[...], hole[...], NT, preferred_element_type=f32)

    def h_sent():
        h1.wait_send()
        drain(hxx.at[pl.ds(1, NX - 1)], h2_ssem.at[0])
        drain(hy.at[pl.ds(1, NY - 1)], h3_ssem.at[0])
        drain(hy.at[pl.ds(1, NY - 1)], h4_ssem.at[0])
        drain(hxx.at[pl.ds(1, NX - 1)], h5_ssem.at[0])
        h6.wait_send()

    def ladder_block(slot):
        return lb[(z + slot) % NZ].reshape(NB, NB)

    def ladder(n, first, step):
        @pl.loop(0, n)
        def _(i):
            slot = (first + step * i) % NZ
            acc[...] += lax.dot_general(m[slot], ladder_block(slot), NT, preferred_element_type=f32)

    def last():
        block = ladder_block(NZ // 2)
        for ch in range(NCH // 2):
            for up in (True, False):
                m_copy(up, NZ // 2 - 1, ch).wait_recv()
                chunk = m_rows(up, ch)
                out[chunk, :] = (acc[chunk, :] + lax.dot_general(
                    m[NZ // 2, chunk], block, NT, preferred_element_type=f32)).astype(bf16)
                pltpu.make_async_copy(out.at[chunk], out_hbm.at[chunk], out_sem.at[0]).start()

    def zm(hop, *chunks):
        for ch in chunks:
            m_forward(hop, ch)

    met("y")
    l0_first()
    met("c")
    h1_send()
    zm(1, 0)
    met("t")
    l0_second()
    m_own(*range(EARLY, NCH))
    met("x")
    h2_send()
    zm(1, 1)
    h3_send()
    l1_send(0)
    zm(1, 2)
    l1_send(2)
    l1_send(6)
    l2_pass(0)
    zm(1, 3)
    h4_send()
    l3_send(0)
    zm(2, 0)
    l1_send(3)
    l1_send(5)
    l1_send(4)
    l2_pass(2)
    zm(2, 1)
    l2_pass(6)
    h5_send()
    l1_send(1)
    l1_send(7)
    l2_pass(3)
    l2_pass(5)
    l2_pass(4)
    zm(2, 2)
    l3_send(1)
    l3_send(7)
    l3_send(2)
    l3_send(6)
    zm(2, 3)
    h6_send()
    l3_send(3)
    l3_send(5)
    l3_send(4)
    zm(3, 0)
    zm(3, 1)
    cycle()
    l3_done()
    ladder(5, 6, 1)
    zm(3, 2, 3)
    ladder(2, 3, 2)
    last()
    drain(out, out_sem.at[0])
    drain(m.at[pl.ds(0, NZ - 1)], m_ssem.at[0])
    l0_sent()
    l_sent()
    h_sent()


def body(amplitudes, tile_mask, ladder_ints, cycle_right, cycle_left):
    dma = pltpu.SemaphoreType.DMA
    return pl.pallas_call(
        kernel,
        out_shape=jax.ShapeDtypeStruct((NB, NB), bf16),
        in_specs=[pl.BlockSpec(memory_space=pl.ANY)] * 5,
        out_specs=pl.BlockSpec(memory_space=pl.ANY),
        scratch_shapes=[
            pltpu.SMEM((NB // TB, NB // TB), jnp.int32),
            pltpu.VMEM((NB, NB), bf16),
            pltpu.VMEM((LC, NB), bf16),
            pltpu.VMEM((NB, NB), bf16),
            pltpu.VMEM((NB, NB), bf16),
            pltpu.VMEM((NZ, NB, NB), bf16),
            pltpu.VMEM((LC, NB), bf16),
            pltpu.VMEM((NZ, NX, 2, LC, NB), bf16),
            pltpu.VMEM((NB, NB), f32),
            pltpu.VMEM((NB, NB), f32),
            pltpu.VMEM((HH, NB), bf16),
            pltpu.VMEM((HH, NB), bf16),
            pltpu.VMEM((HH, NB), bf16),
            pltpu.VMEM((NY, HP, HW), bf16),
            pltpu.VMEM((HQ, NB), bf16),
            pltpu.VMEM((NX, HQ, NB), bf16),
            pltpu.VMEM((NB, NB), bf16),
            pltpu.VMEM((NB, NB), bf16),
            pltpu.SemaphoreType.REGULAR((4 + NX - 1 + NY - 1,)),
            dma((4 + NCH,)),
            dma((1,)),
            dma((1,)), dma((2, NZ // 2 * NCH - NCH // 2)),
            dma((2,)), dma((2,)),
            dma((1,)), dma((NY,)),
            dma((1,)), dma((2, NY)),
            dma((1,)), dma((1,)),
            *[dma((1,))] * 12,
        ],
        compiler_params=pltpu.CompilerParams(
            collective_id=0, has_side_effects=True, vmem_limit_bytes=64 * 2**20),
        cost_estimate=pl.CostEstimate(flops=2 * NB * NB * (NZ * NB + 2 * NB), bytes_accessed=5 * NB * NB * 2, transcendentals=0),
        name="residual_kernel",
    )(tile_mask, amplitudes, ladder_ints.T, cycle_right, cycle_left)


def solution(mesh):
    return jax.shard_map(
        body,
        mesh=mesh,
        in_specs=(
            P("pair", "ka"),
            P("pair", "ka"),
            P("ka", "pair"),
            P("pair", None),
            P("pair", None),
        ),
        out_specs=P("pair", "ka"),
        check_vma=False,
    )
```

```python
import jax
import jax.numpy as jnp
from jax import lax
from jax.experimental import pallas as pl
from jax.experimental.pallas import tpu as pltpu
from jax.sharding import PartitionSpec as P

MESH = pl.DeviceIdType.MESH
TB = 128
NB = 512
NX, NY, NZ = 4, 8, 8
LC = 64
CH = 128
NCH = NB // CH
BESIDE = (1, NY - 1)
EARLY = 2
HH = NB // 2
HQ = HH // NX
HP, HW = HQ // 4, NB // 2

bf16, f32 = jnp.bfloat16, jnp.float32
NT = (((1,), (1,)), ((), ()))
TN = (((0,), (0,)), ((), ()))


def kernel(
    mask_hbm, amp_hbm, lad_hbm, right_hbm, left_hbm, out_hbm,
    mask, amp, lt, right, left, m, la, lb, acc, part, hsend, hx, s1, hy, s2, hxx, hole, out,
    ack, in_sem, out_sem, m_ssem, m_rsem, l0_ssem, l0_rsem, l1_ssem, l1_rsem, l2_ssem, l2_rsem, l3_ssem, l3_rsem,
    h1_ssem, h1_rsem, h2_ssem, h2_rsem, h3_ssem, h3_rsem, h4_ssem, h4_rsem, h5_ssem, h5_rsem, h6_ssem, h6_rsem,
):
    p, z = lax.axis_index("pair"), lax.axis_index("ka")
    c, x, y = p % 2, (p // 2) % NX, p // (2 * NX)
    zt = (y - z + NZ) % NZ

    def dev(dx=0, dy=0, dz=0, dc=0):
        pair = ((y + dy) % NY) * (2 * NX) + ((x + dx) % NX) * 2 + (c + dc) % 2
        return (pair, (z + dz) % NZ)

    def rcopy(src, dst, ssem, rsem, device):
        return pltpu.make_async_remote_copy(
            src_ref=src, dst_ref=dst, send_sem=ssem, recv_sem=rsem, device_id=device, device_id_type=MESH)

    def drain(ref, sem):
        pltpu.make_async_copy(ref, ref, sem).wait()

    def rows(start, size):
        return pl.ds(pl.multiple_of(start, size), size)

    mask_in = pltpu.make_async_copy(mask_hbm, mask, in_sem.at[0])
    inputs = [pltpu.make_async_copy(a, b, in_sem.at[1 + i]) for i, (a, b) in enumerate(
        ((lad_hbm, lt), (right_hbm, right), (left_hbm, left)))]
    amp_in = [pltpu.make_async_copy(amp_hbm.at[pl.ds(i * CH, CH)], amp.at[pl.ds(i * CH, CH)], in_sem.at[4 + i]) for i in range(NCH)]
    from_ends = [i for j in range(NCH // 2) for i in (j, NCH - 1 - j)]
    mask_in.start()
    amp_in[from_ends[0]].start()
    amp_in[from_ends[1]].start()

    def rank(v):
        return jnp.where(v <= NY // 2, 2 * v, 2 * (NY - v) + 1)

    partners = {
        ("z", 1): (dev(dz=1), (z + 1) % NZ > z, None, ("z", -1)),
        ("z", -1): (dev(dz=-1), (z + NZ - 1) % NZ > z, None, ("z", 1)),
        ("t", 0): ((p, zt), zt > z, zt != z, ("t", 0)),
        ("c", 1): (dev(dc=1), c == 1, None, ("c", 1)),
    }
    for d in range(1, NX):
        partners["x", d] = (dev(dx=d), (x + d) % NX > x, None, ("x", NX - d))
    for d in range(1, NY):
        partners["y", d] = (dev(dy=d), rank((y + d) % NY) > rank(y), None, ("y", NY - d))
    ack_of = {name: i for i, name in enumerate(partners)}

    barrier = pltpu.get_barrier_semaphore()
    earlier = 0
    for device, later, valid, _ in partners.values():
        @pl.when(later)
        def _():
            pl.semaphore_signal(barrier, inc=1, device_id=device, device_id_type=MESH)

        before = jnp.logical_not(later)
        if valid is not None:
            before = jnp.logical_and(before, valid)
        earlier += before.astype(jnp.int32)

    def answer():
        @pl.when(earlier > 0)
        def _():
            pl.semaphore_wait(barrier, earlier)

        for device, later, valid, there in partners.values():
            before = jnp.logical_not(later)
            if valid is not None:
                before = jnp.logical_and(before, valid)

            @pl.when(before)
            def _():
                pl.semaphore_signal(ack.at[ack_of[there]], inc=1, device_id=device, device_id_type=MESH)

    def met(axis):
        for name, (_, later, _, _) in partners.items():
            if name[0] == axis:
                @pl.when(later)
                def _():
                    pl.semaphore_wait(ack.at[ack_of[name]], 1)

    for i in from_ends[2:]:
        amp_in[i].start()
    for copy in inputs:
        copy.start()

    def masked(i):
        amp_in[i].wait()
        for v in range(NB // TB):
            here = (slice(i * CH, (i + 1) * CH), slice(v * TB, (v + 1) * TB))
            m[(0, *here)] = (amp[here].astype(f32) * mask[i * CH // TB, v].astype(f32)).astype(bf16)

    answer()
    mask_in.wait()
    masked(from_ends[0])
    masked(from_ends[1])
    met("z")

    def m_rows(up, ch):
        return pl.ds((ch if up else NCH - 1 - ch) * CH, CH)

    def m_copy(up, hop, ch):
        chunk = m_rows(up, ch)
        src, dst = ((NZ - hop) % NZ, NZ - 1 - hop) if up else (hop, hop + 1)
        i = hop * NCH + ch
        return rcopy(m.at[src, chunk], m.at[dst, chunk], m_ssem.at[0], m_rsem.at[int(up), i], dev(dz=1 if up else -1))

    def m_send(up, hop, ch):
        m_copy(up, hop, ch).start()

    def m_forward(hop, ch):
        for up in (True, False):
            m_copy(up, hop - 1, ch).wait_recv()
            if hop < NZ // 2 - 1 or ch < NCH // 2:
                m_send(up, hop, ch)

    def m_own(*chunks):
        for ch in chunks:
            for up in (True, False):
                m_send(up, 0, ch)

    m_own(0)
    for i in range(1, NCH // 2):
        masked(from_ends[2 * i])
        masked(from_ends[2 * i + 1])
        if i < EARLY:
            m_own(i)
    m_own(*range(NCH // 2, EARLY))

    l0a = rcopy(lt, la, l0_ssem.at[0], l0_rsem.at[0], dev(dy=z))
    l0b = rcopy(la, lb.at[z, x, c], l0_ssem.at[1], l0_rsem.at[1], (p, zt))

    def l0_first():
        inputs[0].wait()

        @pl.when(z != 0)
        def _():
            l0a.start()

    def l0_second():
        @pl.when(z != 0)
        def _():
            l0a.wait_recv()

        @pl.when(z == 0)
        def _():
            la[...] = lt[...]

        @pl.when(zt != z)
        def _():
            l0b.start()

        @pl.when(zt == z)
        def _():
            lb[z, x, c] = la[...]

    def l_place(d, dx=0):
        return lb.at[(y - d - z + 2 * NZ) % NZ, (x - dx + NX) % NX, c]

    def l1_copy(d):
        if d == NY // 2:
            src, step = l_place(jnp.where(c == 0, 2, NY - 2)), jnp.where(c == 0, 2, NY - 2)
        else:
            step = {1: 1, 2: 2, 3: 1, 5: NY - 1, 6: NY - 2, 7: NY - 1}[d]
            src = l_place((d - step + NY) % NY)
        return rcopy(src, src, l1_ssem.at[0], l1_rsem.at[d], dev(dy=step))

    def l2_copy(d, dx):
        side = 1 if d % 2 else NX - 1
        src, step = (l_place(d, side), side) if dx == 2 else (l_place(d), dx)
        return rcopy(src, src, l2_ssem.at[0], l2_rsem.at[0 if dx == side else 1, d], dev(dx=step))

    def l2_beside(d, dx):
        return rcopy(l_place(0, dx), l_place(0, dx), l2_ssem.at[0], l2_rsem.at[1, d], dev(dy=d))

    def l3_copy(d):
        there = lb.at[(y - d - z + 2 * NZ) % NZ, :, c]
        return rcopy(there, there, l3_ssem.at[0], l3_rsem.at[0], dev(dc=1))

    def l0_done():
        @pl.when(zt != z)
        def _():
            l0b.wait_recv()

    def l1_send(d):
        if d:
            l1_copy(d).wait_recv()
        else:
            l0_done()
        for further in {0: (1, 7, 2, 6), 2: (3,), 6: (5, 4)}.get(d, ()):
            l1_copy(further).start()
        if d not in BESIDE:
            l2_copy(d, 1).start()
            l2_copy(d, 3).start()

    def l2_pass(d):
        l2_copy(d, 1 if d % 2 else 3).wait_recv()
        l2_copy(d, 2).start()

    def l3_send(d):
        drain(lb.at[0, pl.ds(0, 3 if d in BESIDE else 2), 0], l2_rsem.at[1, d])
        l3_copy(d).start()
        if d == 0:
            for beside in BESIDE:
                for dx in range(1, NX):
                    l2_beside(beside, dx).start()

    def l3_done():
        drain(lb.at[:, :, 0], l3_rsem.at[0])

    def l_sent():
        drain(lb.at[pl.ds(0, NY - 1), 0, 0], l1_ssem.at[0])
        drain(lb.at[:, pl.ds(0, NX - 1), 0], l2_ssem.at[0])
        drain(lb.at[:, :, 0], l3_ssem.at[0])

    def l0_sent():
        @pl.when(z != 0)
        def _():
            l0a.wait_send()

        @pl.when(zt != z)
        def _():
            l0b.wait_send()

    h1 = rcopy(hsend, hx, h1_ssem.at[0], h1_rsem.at[0], dev(dc=1))
    half = rows(c * HH, HH)
    quarter = rows(c * HH + x * HQ, HQ)
    h6 = rcopy(hole.at[half], hole.at[half], h6_ssem.at[0], h6_rsem.at[0], dev(dc=1))

    def piece(v):
        return rows(v // 2 * HP, HP), rows(v % 2 * HW, HW)

    mine = (rows(c * HH + x * HQ + y // 2 * HP, HP), rows(y % 2 * HW, HW))

    def h2_copy(dx):
        return rcopy(s1.at[rows((x + dx) % NX * HQ, HQ)], hxx.at[dx], h2_ssem.at[0], h2_rsem.at[0], dev(dx=dx))

    def h3_copy(d):
        return rcopy(s2.at[piece((y + d) % NY)], hy.at[d], h3_ssem.at[0], h3_rsem.at[0], dev(dy=d))

    def h4_copy(d):
        return rcopy(hole.at[mine], hole.at[mine], h4_ssem.at[0], h4_rsem.at[0], dev(dy=d))

    def h5_copy(dx):
        return rcopy(hole.at[quarter], hole.at[quarter], h5_ssem.at[0], h5_rsem.at[0], dev(dx=dx))

    def h1_send():
        inputs[1].wait()
        part[...] = lax.dot_general(m[0], right[...], TN, preferred_element_type=f32)
        hsend[...] = part[rows((1 - c) * HH, HH), :].astype(bf16)
        h1.start()

    def h2_send():
        h1.wait_recv()
        s1[...] = (part[half, :] + hx[...].astype(f32)).astype(bf16)
        for dx in range(1, NX):
            h2_copy(dx).start()

    def h3_send():
        drain(hxx.at[pl.ds(1, NX - 1)], h2_rsem.at[0])
        total = s1[rows(x * HQ, HQ), :].astype(f32)
        for dx in range(1, NX):
            total += hxx[dx].astype(f32)
        s2[...] = total.astype(bf16)
        for d in range(1, NY):
            h3_copy(d).start()

    def h4_send():
        drain(hy.at[pl.ds(1, NY - 1)], h3_rsem.at[0])
        total = s2[piece(y)].astype(f32)
        for d in range(1, NY):
            total += hy[d].astype(f32)
        hole[mine] = total.astype(bf16)
        for d in range(1, NY):
            h4_copy(d).start()

    def h5_send():
        drain(hy.at[pl.ds(1, NY - 1)], h4_rsem.at[0])
        for dx in range(1, NX):
            h5_copy(dx).start()

    def h6_send():
        drain(hxx.at[pl.ds(1, NX - 1)], h5_rsem.at[0])
        h6.start()

    def cycle():
        h6.wait_recv()
        inputs[2].wait()
        acc[...] = lax.dot_general(left[...], hole[...], NT, preferred_element_type=f32)

    def h_sent():
        h1.wait_send()
        drain(hxx.at[pl.ds(1, NX - 1)], h2_ssem.at[0])
        drain(hy.at[pl.ds(1, NY - 1)], h3_ssem.at[0])
        drain(hy.at[pl.ds(1, NY - 1)], h4_ssem.at[0])
        drain(hxx.at[pl.ds(1, NX - 1)], h5_ssem.at[0])
        h6.wait_send()

    def ladder_block(slot):
        return lb[(z + slot) % NZ].reshape(NB, NB)

    def ladder(n, first, step):
        @pl.loop(0, n)
        def _(i):
            slot = (first + step * i) % NZ
            acc[...] += lax.dot_general(m[slot], ladder_block(slot), NT, preferred_element_type=f32)

    def last():
        block = ladder_block(NZ // 2)
        for ch in range(NCH // 2):
            for up in (True, False):
                m_copy(up, NZ // 2 - 1, ch).wait_recv()
                chunk = m_rows(up, ch)
                out[chunk, :] = (acc[chunk, :] + lax.dot_general(
                    m[NZ // 2, chunk], block, NT, preferred_element_type=f32)).astype(bf16)
                pltpu.make_async_copy(out.at[chunk], out_hbm.at[chunk], out_sem.at[0]).start()

    def zm(hop, *chunks):
        for ch in chunks:
            m_forward(hop, ch)

    met("y")
    l0_first()
    met("c")
    h1_send()
    zm(1, 0)
    met("t")
    l0_second()
    met("x")
    h2_send()
    m_own(*range(EARLY, NCH))
    zm(1, 1)
    h3_send()
    l1_send(0)
    zm(1, 2)
    l1_send(2)
    l1_send(6)
    l2_pass(0)
    zm(1, 3)
    h4_send()
    l3_send(0)
    zm(2, 0)
    l1_send(3)
    l1_send(5)
    l1_send(4)
    l2_pass(2)
    zm(2, 1)
    l2_pass(6)
    h5_send()
    l1_send(1)
    l1_send(7)
    l2_pass(3)
    l2_pass(5)
    l2_pass(4)
    zm(2, 2)
    l3_send(1)
    l3_send(7)
    l3_send(2)
    l3_send(6)
    zm(2, 3)
    h6_send()
    l3_send(3)
    l3_send(5)
    l3_send(4)
    zm(3, 0)
    zm(3, 1)
    cycle()
    l3_done()
    ladder(5, 6, 1)
    zm(3, 2, 3)
    ladder(2, 3, 2)
    last()
    drain(out, out_sem.at[0])
    drain(m.at[pl.ds(0, NZ - 1)], m_ssem.at[0])
    l0_sent()
    l_sent()
    h_sent()


def body(amplitudes, tile_mask, ladder_ints, cycle_right, cycle_left):
    dma = pltpu.SemaphoreType.DMA
    return pl.pallas_call(
        kernel,
        out_shape=jax.ShapeDtypeStruct((NB, NB), bf16),
        in_specs=[pl.BlockSpec(memory_space=pl.ANY)] * 5,
        out_specs=pl.BlockSpec(memory_space=pl.ANY),
        scratch_shapes=[
            pltpu.SMEM((NB // TB, NB // TB), jnp.int32),
            pltpu.VMEM((NB, NB), bf16),
            pltpu.VMEM((LC, NB), bf16),
            pltpu.VMEM((NB, NB), bf16),
            pltpu.VMEM((NB, NB), bf16),
            pltpu.VMEM((NZ, NB, NB), bf16),
            pltpu.VMEM((LC, NB), bf16),
            pltpu.VMEM((NZ, NX, 2, LC, NB), bf16),
            pltpu.VMEM((NB, NB), f32),
            pltpu.VMEM((NB, NB), f32),
            pltpu.VMEM((HH, NB), bf16),
            pltpu.VMEM((HH, NB), bf16),
            pltpu.VMEM((HH, NB), bf16),
            pltpu.VMEM((NY, HP, HW), bf16),
            pltpu.VMEM((HQ, NB), bf16),
            pltpu.VMEM((NX, HQ, NB), bf16),
            pltpu.VMEM((NB, NB), bf16),
            pltpu.VMEM((NB, NB), bf16),
            pltpu.SemaphoreType.REGULAR((4 + NX - 1 + NY - 1,)),
            dma((4 + NCH,)),
            dma((1,)),
            dma((1,)), dma((2, NZ // 2 * NCH - NCH // 2)),
            dma((2,)), dma((2,)),
            dma((1,)), dma((NY,)),
            dma((1,)), dma((2, NY)),
            dma((1,)), dma((1,)),
            *[dma((1,))] * 12,
        ],
        compiler_params=pltpu.CompilerParams(
            collective_id=0, has_side_effects=True, vmem_limit_bytes=64 * 2**20),
        cost_estimate=pl.CostEstimate(flops=2 * NB * NB * (NZ * NB + 2 * NB), bytes_accessed=5 * NB * NB * 2, transcendentals=0),
        name="residual_kernel",
    )(tile_mask, amplitudes, ladder_ints.T, cycle_right, cycle_left)


def solution(mesh):
    return jax.shard_map(
        body,
        mesh=mesh,
        in_specs=(
            P("pair", "ka"),
            P("pair", "ka"),
            P("ka", "pair"),
            P("pair", None),
            P("pair", None),
        ),
        out_specs=P("pair", "ka"),
        check_vma=False,
    )
```
